32 devices in a mesh: group: 2 (over x), wide: 16 (over z, y, core).
Axes of the slice: x: 2, y: 2, z: 4, core: 2. Of those that a mesh axis runs over, the one named last changes fastest.
Arguments:
- basis: bfloat16 [32, 256, 8192], P(('group', 'wide')), parts along dimension 0, may hold values from -0.0625 to 0.0625
- sat_cond: float32 [32, 8192], P(('group', 'wide')), parts along dimension 0, may hold values from 0.1 to 10
- head: float32 [32, 8192], P(('group', 'wide')), parts along dimension 0, may hold values from -2 to 0.5
- storage: float32 [32, 8192], P(('group', 'wide')), parts along dimension 0, may hold values from 0.5 to 4
- counts: int32 [32], P('group'), parts along dimension 0, may hold values from 64 to 256, as said below
- partner: int32 [32], P('group'), parts along dimension 0, may hold values from 0 to 15, as said below
- owner: int32 [32], P('group'), parts along dimension 0, may hold values from 0 to 15, each once
Outputs:
- diag_rows: float32 [32, 256, 256], P(('group', 'wide')), parts along dimension 0
- coupling_rows: float32 [32, 256, 256], P(('group', 'wide')), parts along dimension 0
The draws below stay inside these ranges and needn't reach their ends.
There are 2 independent parts, one for each index of `group`. The reference program is written for one: setup_inputs(seed, part) draws one part's arguments, and reference() takes and returns one part's arrays. A program takes and returns all parts, laid end to end along the dimension named above; each array names one. Nothing has to cross between parts.
Inputs may be any that keep to these rules, and one draw needn't show every extreme that they name: `counts`: some neighbourhood uses all 256 columns and some uses 256 // 4. partner[partner[i]] = i and partner[i] != i. `owner`: each index appears once.
All inputs are finite; a program needn't handle non-finite values.
Results may differ from the reference program's by a relative error of at most 0.0029.
Values may be sent and summed in bfloat16 or wider, within the bound.
A program may use at most 128 MiB of HBM per device.

```python
import math
import jax
import jax.numpy as jnp
from jax import lax

LAT = 64
SLAB = 2
K = 256
OV = 2
NBHD = 16
CELLS = 8192
FACE = 256


def draw_counts(key, part):
    first_key, second_key = jax.random.split(jax.random.fold_in(key, 11))
    drawn = jax.random.randint(first_key, (NBHD,), K // 4, K + 1).astype(jnp.int32)
    order = jax.random.permutation(second_key, NBHD)
    drawn = drawn.at[order[0]].set(K).at[order[1]].set(K // 4)
    return drawn.astype(jnp.int32)


def draw_partner(key, part):
    order = jax.random.permutation(jax.random.fold_in(key, 23), NBHD).astype(jnp.int32)
    firsts = order[0::2]
    seconds = order[1::2]
    paired = jnp.zeros((NBHD,), jnp.int32).at[firsts].set(seconds).at[seconds].set(firsts)
    return paired.astype(jnp.int32)


def steps_of(key, shape, shards, low, largest):
    def one(axis_at, blocks):
        steps = jax.random.uniform(jax.random.fold_in(jax.random.fold_in(key, 6), axis_at), (blocks,), jnp.float32, low / len(shards), largest / len(shards))
        return jnp.repeat(jnp.exp(steps), shape[axis_at] // blocks).reshape((-1,) + (1,) * (len(shape) - axis_at - 1))

    gain = one(*shards[0])
    for cut in shards[1:]:
        gain = gain * one(*cut)
    return gain


def scatter_about(key, dims, spread, most, cuts=(), held_as=jnp.bfloat16):
    array = jax.random.normal(key, dims, jnp.float32) * spread
    if len(cuts) > 0:
        array = steps_of(key, dims, cuts, -0.22, 0.18) * array
    return jnp.clip(array, min=-most, max=most).astype(held_as)


def setup_inputs(seed: int = 0, part: int = 0) -> dict:
    key_of = jax.random.split(jax.random.key(seed), 8)
    own_keys = jax.random.split(jax.random.fold_in(key_of[7], part), 8)
    basis = scatter_about(own_keys[0], (NBHD, K, CELLS), CELLS ** -0.5, 0.0625, ((0, 16),))
    sat_cond = jnp.clip(jnp.exp(math.log(10.0) - 4.6051702 * jax.random.uniform(own_keys[1], (NBHD, CELLS), jnp.float32) ** steps_of(own_keys[1], (NBHD, CELLS), ((0, 16),), -0.2, 0.2)), 0.1, 10.0)
    head = jnp.clip(-2.0 + 2.5 * jax.random.uniform(own_keys[2], (NBHD, CELLS), jnp.float32) ** steps_of(own_keys[2], (NBHD, CELLS), ((0, 16),), -0.2, 0.2), -2.0, 0.5)
    storage = jnp.clip(jnp.exp(math.log(4.0) - 2.0794415 * jax.random.uniform(own_keys[3], (NBHD, CELLS), jnp.float32) ** steps_of(own_keys[3], (NBHD, CELLS), ((0, 16),), -0.2, 0.2)), 0.5, 4.0)
    counts = draw_counts(jax.random.fold_in(jax.random.fold_in(key_of[7], part), 71), part)
    partner = draw_partner(jax.random.fold_in(jax.random.fold_in(key_of[7], part), 71), part)
    owner = jax.random.permutation(own_keys[6], NBHD).astype(jnp.int32)
    return {"basis": basis, "sat_cond": sat_cond, "head": head, "storage": storage, "counts": counts, "partner": partner, "owner": owner}


def harmonic(first, second):
    return 2.0 * first * second / (first + second)


def stencil_image(masked, conduct, stored):
    values = masked.astype(jnp.float32)
    result = stored * values
    trans_x = harmonic(conduct[:, :, 1:], conduct[:, :, :-1])
    flux_x = trans_x * (values[..., 1:] - values[..., :-1])
    result = result + jnp.pad(flux_x, ((0, 0), (0, 0), (0, 0), (1, 0))) - jnp.pad(flux_x, ((0, 0), (0, 0), (0, 0), (0, 1)))
    trans_y = harmonic(conduct[:, 1:, :], conduct[:, :-1, :])
    flux_y = trans_y * (values[:, :, 1:, :] - values[:, :, :-1, :])
    result = result + jnp.pad(flux_y, ((0, 0), (0, 0), (1, 0), (0, 0))) - jnp.pad(flux_y, ((0, 0), (0, 0), (0, 1), (0, 0)))
    trans_z = harmonic(conduct[1:, :, :], conduct[:-1, :, :])
    flux_z = trans_z * (values[:, 1:, :, :] - values[:, :-1, :, :])
    result = result + jnp.pad(flux_z, ((0, 0), (1, 0), (0, 0), (0, 0))) - jnp.pad(flux_z, ((0, 0), (0, 1), (0, 0), (0, 0)))
    return result.astype(jnp.bfloat16)


def reference(basis, sat_cond, head, storage, counts, partner, owner):
    row_iota = jnp.arange(K, dtype=jnp.int32)
    zero_half = jnp.zeros((), jnp.bfloat16)
    west_all = basis.reshape(NBHD, K, SLAB, LAT, LAT)[..., :OV].reshape(NBHD, K, FACE)
    west_all = jnp.where(row_iota[None, :, None] < counts[:, None, None], west_all, zero_half)

    def one_block(index):
        masked = jnp.where(row_iota[:, None] < counts[index], basis[index], zero_half)
        conduct = (sat_cond[index] * jnp.exp(head[index])).reshape(SLAB, LAT, LAT)
        stored = storage[index].reshape(SLAB, LAT, LAT)
        image = stencil_image(masked.reshape(K, SLAB, LAT, LAT), conduct, stored).reshape(K, CELLS)
        diag_block = lax.dot_general(masked, image, (((1,), (1,)), ((), ())), preferred_element_type=jnp.float32)
        east = image.reshape(K, SLAB, LAT, LAT)[..., LAT - OV:].reshape(K, FACE)
        facing = west_all[partner[index]]
        coupling = lax.dot_general(east, facing, (((1,), (1,)), ((), ())), preferred_element_type=jnp.float32)
        return diag_block, coupling

    diag_blocks, couplings = lax.map(one_block, jnp.arange(NBHD, dtype=jnp.int32))
    diag_rows = jnp.zeros_like(diag_blocks).at[owner].set(diag_blocks)
    coupling_rows = jnp.zeros_like(couplings).at[owner].set(couplings)
    return (diag_rows, coupling_rows)
```

```python
import functools

import jax
import jax.numpy as jnp
from jax import lax
from jax.experimental import pallas as pl
from jax.experimental.pallas import tpu as pltpu
from jax.sharding import PartitionSpec as P

LAT = 64
SLAB = 2
FACE = 256
LANES = 128
ROWS = 16
TILES = LAT * LAT // LANES
GROUP = 16
HALVES = 2


def harmonic(first, second):
    return 2.0 * first * second / (first + second)


def tile_of(plane, tile):
    start = plane * LAT * LAT + tile * LANES
    return slice(start, start + LANES)


def coefficients(sat_ref, head_ref, storage_ref, coef_ref):
    lane = lax.broadcasted_iota(jnp.int32, (8, LANES), 1)
    low = lane < LAT
    inside = lane % LAT != LAT - 1

    def wide(ref, plane, tile):
        return jnp.broadcast_to(ref[0:1, tile_of(plane, tile)], (8, LANES))

    conduct = [
        [wide(sat_ref, z, j) * jnp.exp(wide(head_ref, z, j)) for j in range(TILES)]
        for z in range(SLAB)
    ]
    for j in range(TILES):
        along_z = harmonic(conduct[0][j], conduct[1][j])
        for z in range(SLAB):
            own = conduct[z][j]
            right = jnp.where(inside, harmonic(own, pltpu.roll(own, LANES - 1, 1)), 0.0)
            left = pltpu.roll(right, 1, 1)
            within = harmonic(own, pltpu.roll(own, LAT, 1))
            before = pltpu.roll(conduct[z][max(j - 1, 0)], LAT, 1)
            after = pltpu.roll(conduct[z][min(j + 1, TILES - 1)], LAT, 1)
            across = harmonic(own, jnp.where(low, before, after))
            if j == 0:
                across = jnp.where(low, 0.0, across)
            if j == TILES - 1:
                across = jnp.where(low, across, 0.0)
            total = wide(storage_ref, z, j) + right + left + within + across + along_z
            for n, value in enumerate((total, right, left, within, across, along_z)):
                coef_ref[n, :, tile_of(z, j)] = value


def kernel(
    width,
    piece_rows,
    basis_ref,
    sat_ref,
    head_ref,
    storage_ref,
    counts_ref,
    partner_ref,
    owner_ref,
    diag_ref,
    coupling_ref,
    basis_v,
    image_v,
    coef_ref,
    face_src,
    face_recv,
    face_stage,
    face_fin,
    diag_src,
    diag_recv_0,
    diag_recv_1,
    diag_stage,
    diag_fin,
    inverse_ref,
    load_sem,
    face_sems,
    diag_sems,
):
    diag_recv = (diag_recv_0, diag_recv_1)
    rows_total = basis_v.shape[0]
    pieces = rows_total // piece_rows
    stride = width // pieces
    half_rows = rows_total // HALVES
    me = lax.axis_index("wide")
    own_piece = me // stride
    is_middle = lax.rem(me, stride) == 0

    loads = []
    for h in range(HALVES):
        part = pl.ds(h * half_rows, half_rows)
        loads.append(
            pltpu.make_async_copy(basis_ref.at[0, part], basis_v.at[part], load_sem.at[h])
        )
        loads[-1].start()

    barrier = pltpu.get_barrier_semaphore()

    @pl.loop(1, width)
    def _(step):
        pl.semaphore_signal(
            barrier,
            inc=1,
            device_id={"wide": lax.rem(me + step, width)},
            device_id_type=pl.DeviceIdType.MESH,
        )

    coefficients(sat_ref, head_ref, storage_ref, coef_ref)

    @pl.loop(0, width)
    def _(d):
        found = jnp.int32(0)
        for i in range(width):
            found = jnp.where(owner_ref[i] == d, i, found)
        inverse_ref[d] = found

    pl.semaphore_wait(barrier, width - 1)

    own_count = counts_ref[me]
    lane = lax.broadcasted_iota(jnp.int32, (ROWS, LANES), 1)
    low = lane < LAT
    westerly = lane % LAT < 2

    def copy_to(src, dst, send_sem, recv_sem, target):
        return pltpu.make_async_remote_copy(
            src_ref=src,
            dst_ref=dst,
            send_sem=send_sem,
            recv_sem=recv_sem,
            device_id={"wide": target},
            device_id_type=pl.DeviceIdType.MESH,
        )

    def first_leg(src, recv, sems, piece):
        target = piece * stride
        return copy_to(
            src.at[piece], recv.at[me], sems.at[0, piece], sems.at[1, me], target
        )

    def second_leg(stage, fin, sems, target):
        return copy_to(
            stage.at[target],
            fin.at[own_piece],
            sems.at[2, target],
            sems.at[3, own_piece],
            target,
        )

    groups_per_piece = piece_rows // ROWS

    def image_group(half, step):
        groups = half_rows // ROWS
        local_group = lax.rem(step + me * groups_per_piece, groups)
        row = pl.multiple_of(half * half_rows + local_group * ROWS, ROWS)
        keep = row + lax.broadcasted_iota(jnp.int32, (ROWS, LANES), 0) < own_count
        values = {}
        turned = {}

        def value(z, j):
            if (z, j) not in values:
                values[z, j] = basis_v[pl.ds(row, ROWS), tile_of(z, j)].astype(jnp.float32)
            return values[z, j]

        def turn(z, j):
            j = min(max(j, 0), TILES - 1)
            if (z, j) not in turned:
                turned[z, j] = pltpu.roll(value(z, j), LAT, 1)
            return turned[z, j]

        def coef(n, z, j):
            one = coef_ref[n, :, tile_of(z, j)]
            return jnp.concatenate([one] * (ROWS // 8), axis=0)

        faces = [[None] * (TILES // GROUP) for _ in range(SLAB)]
        for j in range(TILES):
            along_z = coef(5, 0, j)
            shift = 4 * (j % GROUP)
            landing = (lane - (LAT - 2) - shift + LANES) % LAT < 4
            for z in range(SLAB):
                own = value(z, j)
                image = coef(0, z, j) * own
                image = image - coef(1, z, j) * pltpu.roll(own, LANES - 1, 1)
                image = image - coef(2, z, j) * pltpu.roll(own, 1, 1)
                image = image - coef(3, z, j) * turn(z, j)
                image = image - coef(4, z, j) * jnp.where(low, turn(z, j - 1), turn(z, j + 1))
                image = image - along_z * value(1 - z, j)
                image_v[pl.ds(pl.multiple_of(local_group * ROWS, ROWS), ROWS), tile_of(z, j)] = (
                    image.astype(jnp.bfloat16)
                )
                mixed = jnp.where(westerly, own, image)
                if shift:
                    mixed = pltpu.roll(mixed, shift, 1)
                held = faces[z][j // GROUP]
                faces[z][j // GROUP] = mixed if held is None else jnp.where(landing, mixed, held)
        piece = row // piece_rows
        place = pl.multiple_of(lax.rem(row, piece_rows), ROWS)
        flat = [tile for plane in faces for tile in plane]
        for n, tile in enumerate(flat):
            face_src[piece, pl.ds(place, ROWS), n * LANES : (n + 1) * LANES] = jnp.where(
                keep, tile, 0.0
            ).astype(jnp.bfloat16)
        return piece

    def image_half(half):
        piece_per_half = pieces // HALVES

        @pl.loop(0, piece_per_half)
        def _(step):
            piece = None
            for part in range(groups_per_piece):
                piece = image_group(half, step * groups_per_piece + part)

            @pl.when(piece * stride != me)
            def _():
                first_leg(face_src, face_recv, face_sems, piece).start()

            @pl.when(piece * stride == me)
            def _():
                face_recv[me] = face_src[piece]

    def diag_half(half):
        block = lax.dot_general(
            basis_v[...], image_v[...], (((1,), (1,)), ((), ())), preferred_element_type=jnp.float32
        )
        row = lax.broadcasted_iota(jnp.int32, block.shape, 0)
        column = lax.broadcasted_iota(jnp.int32, block.shape, 1) + half * half_rows
        block = jnp.where((row < own_count) & (column < own_count), block, 0.0)
        diag_src[half] = block.astype(jnp.bfloat16).reshape(pieces, piece_rows, half_rows)

        @pl.loop(0, pieces)
        def _(step):
            piece = lax.rem(step + own_piece, pieces)

            @pl.when(piece * stride != me)
            def _():
                first_leg(diag_src.at[half], diag_recv[half], diag_sems.at[half], piece).start()

            @pl.when(piece * stride == me)
            def _():
                diag_recv[half][me] = diag_src[half, piece]

    def wait_first(src, recv, sems):
        @pl.loop(0, width)
        def _(source):
            @pl.when(source != me)
            def _():
                copy_to(
                    src.at[own_piece], recv.at[source], sems.at[0, own_piece], sems.at[1, source], source
                ).wait_recv()

    def wait_second(stage, fin, sems):
        @pl.loop(0, pieces)
        def _(piece):
            @pl.when(piece * stride != me)
            def _():
                copy_to(
                    stage.at[me], fin.at[piece], sems.at[2, me], sems.at[3, piece], piece * stride
                ).wait_recv()

    def forward(pick, src, recv, stage, fin, sems):
        @pl.when(is_middle)
        def _():
            wait_first(src, recv, sems)

            @pl.loop(1, width + 1)
            def _(step):
                target = lax.rem(me + step, width)
                taken = pick(inverse_ref[target])

                @pl.when(target != me)
                def _():
                    stage[target] = taken
                    second_leg(stage, fin, sems, target).start()

                @pl.when(target == me)
                def _():
                    fin[own_piece] = taken

    def wait_sent(src, recv, stage, fin, sems):
        @pl.loop(0, pieces)
        def _(piece):
            @pl.when(piece * stride != me)
            def _():
                first_leg(src, recv, sems, piece).wait_send()

        @pl.when(is_middle)
        def _():
            @pl.loop(0, width)
            def _(target):
                @pl.when(target != me)
                def _():
                    second_leg(stage, fin, sems, target).wait_send()

    face_lane = lax.broadcasted_iota(jnp.int32, (piece_rows, 2 * FACE), 1)
    easterly = face_lane % 4 >= 2

    def pick_face(source):
        east = face_recv[source].astype(jnp.float32)
        west = face_recv[partner_ref[source]].astype(jnp.float32)
        return jnp.where(easterly, east, west).astype(jnp.bfloat16)

    loads[0].wait()
    image_half(0)
    loads[1].wait()
    diag_half(0)
    image_half(1)
    diag_half(1)
    face_refs = (face_src, face_recv, face_stage, face_fin, face_sems)
    diag_refs = [
        (diag_src.at[h], diag_recv[h], diag_stage.at[h], diag_fin.at[h], diag_sems.at[h])
        for h in range(HALVES)
    ]
    forward(pick_face, *face_refs)
    for h in range(HALVES):
        forward(lambda source, h=h: diag_recv[h][source], *diag_refs[h])

    wait_second(face_stage, face_fin, face_sems)
    both = face_fin[...].reshape(rows_total, 2 * FACE).astype(jnp.float32)
    easts, wests = [], []
    east_lane = lax.broadcasted_iota(jnp.int32, (rows_total, LANES), 1) % 4 >= 2
    for n in range(2 * FACE // LANES):
        tile = both[:, n * LANES : (n + 1) * LANES]
        easts.append(jnp.where(east_lane, tile, 0.0).astype(jnp.bfloat16))
        wests.append(pltpu.roll(tile, LAT - 2, 1).astype(jnp.bfloat16))
    coupling_ref[0] = lax.dot_general(
        jnp.concatenate(easts, axis=1),
        jnp.concatenate(wests, axis=1),
        (((1,), (1,)), ((), ())),
        preferred_element_type=jnp.float32,
    )
    for h in range(HALVES):
        wait_second(diag_stage.at[h], diag_fin.at[h], diag_sems.at[h])
        diag_ref[0, :, h * half_rows : (h + 1) * half_rows] = (
            diag_fin[h].reshape(rows_total, half_rows).astype(jnp.float32)
        )
    wait_sent(*face_refs)
    for h in range(HALVES):
        wait_sent(*diag_refs[h])


def local(width, basis, sat_cond, head, storage, counts, partner, owner):
    rows = basis.shape[1]
    cells = basis.shape[2]
    piece_rows = max(ROWS, rows // width)
    pieces = rows // piece_rows
    half = rows // HALVES
    bf16 = jnp.bfloat16
    out = jax.ShapeDtypeStruct((1, rows, rows), jnp.float32)
    vmem = pl.BlockSpec(memory_space=pltpu.VMEM)
    smem = pl.BlockSpec(memory_space=pltpu.SMEM)
    return pl.pallas_call(
        functools.partial(kernel, width, piece_rows),
        out_shape=(out, out),
        in_specs=[pl.BlockSpec(memory_space=pl.ANY), vmem, vmem, vmem, smem, smem, smem],
        out_specs=(vmem, vmem),
        scratch_shapes=[
            pltpu.VMEM((rows, cells), bf16),
            pltpu.VMEM((half, cells), bf16),
            pltpu.VMEM((6, 8, cells), jnp.float32),
            pltpu.VMEM((pieces, piece_rows, 2 * FACE), bf16),
            pltpu.VMEM((width, piece_rows, 2 * FACE), bf16),
            pltpu.VMEM((width, piece_rows, 2 * FACE), bf16),
            pltpu.VMEM((pieces, piece_rows, 2 * FACE), bf16),
            pltpu.VMEM((HALVES, pieces, piece_rows, half), bf16),
            pltpu.VMEM((width, piece_rows, half), bf16),
            pltpu.VMEM((width, piece_rows, half), bf16),
            pltpu.VMEM((HALVES, width, piece_rows, half), bf16),
            pltpu.VMEM((HALVES, pieces, piece_rows, half), bf16),
            pltpu.SMEM((width,), jnp.int32),
            pltpu.SemaphoreType.DMA((HALVES,)),
            pltpu.SemaphoreType.DMA((4, width)),
            pltpu.SemaphoreType.DMA((HALVES, 4, width)),
        ],
        compiler_params=pltpu.CompilerParams(
            collective_id=0, has_side_effects=True, vmem_limit_bytes=40 * 1024 * 1024
        ),
    )(basis, sat_cond, head, storage, counts, partner, owner)


def solution(mesh):
    placed = (
        P(("group", "wide"), None, None),
        P(("group", "wide"), None),
        P(("group", "wide"), None),
        P(("group", "wide"), None),
        P("group"),
        P("group"),
        P("group"),
    )
    return jax.shard_map(
        functools.partial(local, mesh.shape["wide"]),
        mesh=mesh,
        in_specs=placed,
        out_specs=(P(("group", "wide"), None, None), P(("group", "wide"), None, None)),
        check_vma=False,
    )
```

```python
import functools

import jax
import jax.numpy as jnp
from jax import lax
from jax.experimental import pallas as pl
from jax.experimental.pallas import tpu as pltpu
from jax.sharding import PartitionSpec as P

LAT = 64
SLAB = 2
FACE = 256
LANES = 128
ROWS = 16
TILES = LAT * LAT // LANES
GROUP = 16
HALVES = 2


def harmonic(first, second):
    return 2.0 * first * second / (first + second)


def tile_of(plane, tile):
    start = plane * LAT * LAT + tile * LANES
    return slice(start, start + LANES)


def coefficients(sat_ref, head_ref, storage_ref, coef_ref):
    lane = lax.broadcasted_iota(jnp.int32, (8, LANES), 1)
    low = lane < LAT
    inside = lane % LAT != LAT - 1

    def wide(ref, plane, tile):
        return jnp.broadcast_to(ref[0:1, tile_of(plane, tile)], (8, LANES))

    conduct = [
        [wide(sat_ref, z, j) * jnp.exp(wide(head_ref, z, j)) for j in range(TILES)]
        for z in range(SLAB)
    ]
    for j in range(TILES):
        along_z = harmonic(conduct[0][j], conduct[1][j])
        for z in range(SLAB):
            own = conduct[z][j]
            right = jnp.where(inside, harmonic(own, pltpu.roll(own, LANES - 1, 1)), 0.0)
            left = pltpu.roll(right, 1, 1)
            within = harmonic(own, pltpu.roll(own, LAT, 1))
            before = pltpu.roll(conduct[z][max(j - 1, 0)], LAT, 1)
            after = pltpu.roll(conduct[z][min(j + 1, TILES - 1)], LAT, 1)
            across = harmonic(own, jnp.where(low, before, after))
            if j == 0:
                across = jnp.where(low, 0.0, across)
            if j == TILES - 1:
                across = jnp.where(low, across, 0.0)
            total = wide(storage_ref, z, j) + right + left + within + across + along_z
            for n, value in enumerate((total, right, left, within, across, along_z)):
                coef_ref[n, :, tile_of(z, j)] = value


def kernel(
    width,
    piece_rows,
    basis_ref,
    sat_ref,
    head_ref,
    storage_ref,
    counts_ref,
    partner_ref,
    owner_ref,
    diag_ref,
    coupling_ref,
    basis_v,
    image_v,
    coef_ref,
    face_src,
    face_recv,
    face_stage,
    face_fin,
    diag_src,
    diag_recv_0,
    diag_recv_1,
    diag_stage,
    diag_fin,
    inverse_ref,
    load_sem,
    face_sems,
    diag_sems,
):
    diag_recv = (diag_recv_0, diag_recv_1)
    rows_total = basis_v.shape[0]
    pieces = rows_total // piece_rows
    stride = width // pieces
    half_rows = rows_total // HALVES
    me = lax.axis_index("wide")
    own_piece = me // stride
    is_middle = lax.rem(me, stride) == 0

    loads = []
    for h in range(HALVES):
        part = pl.ds(h * half_rows, half_rows)
        loads.append(
            pltpu.make_async_copy(basis_ref.at[0, part], basis_v.at[part], load_sem.at[h])
        )
        loads[-1].start()

    barrier = pltpu.get_barrier_semaphore()

    @pl.loop(1, width)
    def _(step):
        pl.semaphore_signal(
            barrier,
            inc=1,
            device_id={"wide": lax.rem(me + step, width)},
            device_id_type=pl.DeviceIdType.MESH,
        )

    coefficients(sat_ref, head_ref, storage_ref, coef_ref)

    @pl.loop(0, width)
    def _(d):
        found = jnp.int32(0)
        for i in range(width):
            found = jnp.where(owner_ref[i] == d, i, found)
        inverse_ref[d] = found

    pl.semaphore_wait(barrier, width - 1)

    own_count = counts_ref[me]
    lane = lax.broadcasted_iota(jnp.int32, (ROWS, LANES), 1)
    low = lane < LAT
    westerly = lane % LAT < 2

    def copy_to(src, dst, send_sem, recv_sem, target):
        return pltpu.make_async_remote_copy(
            src_ref=src,
            dst_ref=dst,
            send_sem=send_sem,
            recv_sem=recv_sem,
            device_id={"wide": target},
            device_id_type=pl.DeviceIdType.MESH,
        )

    def first_leg(src, recv, sems, piece):
        target = piece * stride
        return copy_to(
            src.at[piece], recv.at[me], sems.at[0, piece], sems.at[1, me], target
        )

    def second_leg(stage, fin, sems, target):
        return copy_to(
            stage.at[target],
            fin.at[own_piece],
            sems.at[2, target],
            sems.at[3, own_piece],
            target,
        )

    groups_per_piece = piece_rows // ROWS

    def group_rows(half, step):
        local_group = lax.rem(step + me * groups_per_piece, half_rows // ROWS)
        place = pl.multiple_of(local_group * ROWS, ROWS)
        return place, pl.multiple_of(half * half_rows + place, ROWS)

    def image_group(half, step):
        place, row = group_rows(half, step)
        values = {}
        turned = {}

        def value(z, j):
            if (z, j) not in values:
                values[z, j] = basis_v[pl.ds(row, ROWS), tile_of(z, j)].astype(jnp.float32)
            return values[z, j]

        def turn(z, j):
            j = min(max(j, 0), TILES - 1)
            if (z, j) not in turned:
                turned[z, j] = pltpu.roll(value(z, j), LAT, 1)
            return turned[z, j]

        def coef(n, z, j):
            one = coef_ref[n, :, tile_of(z, j)]
            return jnp.concatenate([one] * (ROWS // 8), axis=0)

        for j in range(TILES):
            along_z = coef(5, 0, j)
            for z in range(SLAB):
                own = value(z, j)
                image = coef(0, z, j) * own
                image = image - coef(1, z, j) * pltpu.roll(own, LANES - 1, 1)
                image = image - coef(2, z, j) * pltpu.roll(own, 1, 1)
                image = image - coef(3, z, j) * turn(z, j)
                image = image - coef(4, z, j) * jnp.where(low, turn(z, j - 1), turn(z, j + 1))
                image = image - along_z * value(1 - z, j)
                image_v[pl.ds(place, ROWS), tile_of(z, j)] = image.astype(jnp.bfloat16)

    def face_group(half, step):
        place, row = group_rows(half, step)
        keep = row + lax.broadcasted_iota(jnp.int32, (ROWS, LANES), 0) < own_count
        piece = row // piece_rows
        inner = pl.multiple_of(lax.rem(row, piece_rows), ROWS)
        for z in range(SLAB):
            for first in range(0, TILES, GROUP):
                held = None
                for j in range(first, first + GROUP):
                    shift = 4 * (j % GROUP)
                    landing = (lane - (LAT - 2) - shift + LANES) % LAT < 4
                    mixed = jnp.where(
                        westerly,
                        basis_v[pl.ds(row, ROWS), tile_of(z, j)].astype(jnp.float32),
                        image_v[pl.ds(place, ROWS), tile_of(z, j)].astype(jnp.float32),
                    )
                    if shift:
                        mixed = pltpu.roll(mixed, shift, 1)
                    held = mixed if held is None else jnp.where(landing, mixed, held)
                n = (z * TILES + first) // GROUP
                face_src[piece, pl.ds(inner, ROWS), n * LANES : (n + 1) * LANES] = jnp.where(
                    keep, held, 0.0
                ).astype(jnp.bfloat16)
        return piece

    def image_half(half):
        piece_per_half = pieces // HALVES

        @pl.loop(0, half_rows // ROWS)
        def _(step):
            image_group(half, step)

        @pl.loop(0, piece_per_half)
        def _(step):
            piece = None
            for part in range(groups_per_piece):
                piece = face_group(half, step * groups_per_piece + part)

            @pl.when(piece * stride != me)
            def _():
                first_leg(face_src, face_recv, face_sems, piece).start()

            @pl.when(piece * stride == me)
            def _():
                face_recv[me] = face_src[piece]

    def diag_half(half):
        block = lax.dot_general(
            basis_v[...], image_v[...], (((1,), (1,)), ((), ())), preferred_element_type=jnp.float32
        )
        row = lax.broadcasted_iota(jnp.int32, block.shape, 0)
        column = lax.broadcasted_iota(jnp.int32, block.shape, 1) + half * half_rows
        block = jnp.where((row < own_count) & (column < own_count), block, 0.0)
        diag_src[half] = block.astype(jnp.bfloat16).reshape(pieces, piece_rows, half_rows)

        @pl.loop(0, pieces)
        def _(step):
            piece = lax.rem(step + own_piece, pieces)

            @pl.when(piece * stride != me)
            def _():
                first_leg(diag_src.at[half], diag_recv[half], diag_sems.at[half], piece).start()

            @pl.when(piece * stride == me)
            def _():
                diag_recv[half][me] = diag_src[half, piece]

    def wait_first(src, recv, sems):
        @pl.loop(0, width)
        def _(source):
            @pl.when(source != me)
            def _():
                copy_to(
                    src.at[own_piece], recv.at[source], sems.at[0, own_piece], sems.at[1, source], source
                ).wait_recv()

    def wait_second(stage, fin, sems):
        @pl.loop(0, pieces)
        def _(piece):
            @pl.when(piece * stride != me)
            def _():
                copy_to(
                    stage.at[me], fin.at[piece], sems.at[2, me], sems.at[3, piece], piece * stride
                ).wait_recv()

    def forward(pick, src, recv, stage, fin, sems):
        @pl.when(is_middle)
        def _():
            wait_first(src, recv, sems)

            @pl.loop(1, width + 1)
            def _(step):
                target = lax.rem(me + step, width)
                taken = pick(inverse_ref[target])

                @pl.when(target != me)
                def _():
                    stage[target] = taken
                    second_leg(stage, fin, sems, target).start()

                @pl.when(target == me)
                def _():
                    fin[own_piece] = taken

    def wait_sent(src, recv, stage, fin, sems):
        @pl.loop(0, pieces)
        def _(piece):
            @pl.when(piece * stride != me)
            def _():
                first_leg(src, recv, sems, piece).wait_send()

        @pl.when(is_middle)
        def _():
            @pl.loop(0, width)
            def _(target):
                @pl.when(target != me)
                def _():
                    second_leg(stage, fin, sems, target).wait_send()

    face_lane = lax.broadcasted_iota(jnp.int32, (piece_rows, 2 * FACE), 1)
    easterly = face_lane % 4 >= 2

    def pick_face(source):
        east = face_recv[source].astype(jnp.float32)
        west = face_recv[partner_ref[source]].astype(jnp.float32)
        return jnp.where(easterly, east, west).astype(jnp.bfloat16)

    loads[0].wait()
    image_half(0)
    loads[1].wait()
    diag_half(0)
    image_half(1)
    diag_half(1)
    face_refs = (face_src, face_recv, face_stage, face_fin, face_sems)
    diag_refs = [
        (diag_src.at[h], diag_recv[h], diag_stage.at[h], diag_fin.at[h], diag_sems.at[h])
        for h in range(HALVES)
    ]
    forward(pick_face, *face_refs)
    for h in range(HALVES):
        forward(lambda source, h=h: diag_recv[h][source], *diag_refs[h])

    wait_second(face_stage, face_fin, face_sems)
    both = face_fin[...].reshape(rows_total, 2 * FACE).astype(jnp.float32)
    easts, wests = [], []
    east_lane = lax.broadcasted_iota(jnp.int32, (rows_total, LANES), 1) % 4 >= 2
    for n in range(2 * FACE // LANES):
        tile = both[:, n * LANES : (n + 1) * LANES]
        easts.append(jnp.where(east_lane, tile, 0.0).astype(jnp.bfloat16))
        wests.append(pltpu.roll(tile, LAT - 2, 1).astype(jnp.bfloat16))
    coupling_ref[0] = lax.dot_general(
        jnp.concatenate(easts, axis=1),
        jnp.concatenate(wests, axis=1),
        (((1,), (1,)), ((), ())),
        preferred_element_type=jnp.float32,
    )
    for h in range(HALVES):
        wait_second(diag_stage.at[h], diag_fin.at[h], diag_sems.at[h])
        diag_ref[0, :, h * half_rows : (h + 1) * half_rows] = (
            diag_fin[h].reshape(rows_total, half_rows).astype(jnp.float32)
        )
    wait_sent(*face_refs)
    for h in range(HALVES):
        wait_sent(*diag_refs[h])


def local(width, basis, sat_cond, head, storage, counts, partner, owner):
    rows = basis.shape[1]
    cells = basis.shape[2]
    piece_rows = max(ROWS, rows // width)
    pieces = rows // piece_rows
    half = rows // HALVES
    bf16 = jnp.bfloat16
    out = jax.ShapeDtypeStruct((1, rows, rows), jnp.float32)
    vmem = pl.BlockSpec(memory_space=pltpu.VMEM)
    smem = pl.BlockSpec(memory_space=pltpu.SMEM)
    return pl.pallas_call(
        functools.partial(kernel, width, piece_rows),
        out_shape=(out, out),
        in_specs=[pl.BlockSpec(memory_space=pl.ANY), vmem, vmem, vmem, smem, smem, smem],
        out_specs=(vmem, vmem),
        scratch_shapes=[
            pltpu.VMEM((rows, cells), bf16),
            pltpu.VMEM((half, cells), bf16),
            pltpu.VMEM((6, 8, cells), jnp.float32),
            pltpu.VMEM((pieces, piece_rows, 2 * FACE), bf16),
            pltpu.VMEM((width, piece_rows, 2 * FACE), bf16),
            pltpu.VMEM((width, piece_rows, 2 * FACE), bf16),
            pltpu.VMEM((pieces, piece_rows, 2 * FACE), bf16),
            pltpu.VMEM((HALVES, pieces, piece_rows, half), bf16),
            pltpu.VMEM((width, piece_rows, half), bf16),
            pltpu.VMEM((width, piece_rows, half), bf16),
            pltpu.VMEM((HALVES, width, piece_rows, half), bf16),
            pltpu.VMEM((HALVES, pieces, piece_rows, half), bf16),
            pltpu.SMEM((width,), jnp.int32),
            pltpu.SemaphoreType.DMA((HALVES,)),
            pltpu.SemaphoreType.DMA((4, width)),
            pltpu.SemaphoreType.DMA((HALVES, 4, width)),
        ],
        compiler_params=pltpu.CompilerParams(
            collective_id=0, has_side_effects=True, vmem_limit_bytes=60 * 1024 * 1024
        ),
    )(basis, sat_cond, head, storage, counts, partner, owner)


def solution(mesh):
    placed = (
        P(("group", "wide"), None, None),
        P(("group", "wide"), None),
        P(("group", "wide"), None),
        P(("group", "wide"), None),
        P("group"),
        P("group"),
        P("group"),
    )
    return jax.shard_map(
        functools.partial(local, mesh.shape["wide"]),
        mesh=mesh,
        in_specs=placed,
        out_specs=(P(("group", "wide"), None, None), P(("group", "wide"), None, None)),
        check_vma=False,
    )
```

```python
import functools

import jax
import jax.numpy as jnp
from jax import lax
from jax.experimental import pallas as pl
from jax.experimental.pallas import tpu as pltpu
from jax.sharding import PartitionSpec as P

LAT = 64
SLAB = 2
FACE = 256
LANES = 128
ROWS = 16
TILES = LAT * LAT // LANES
GROUP = 16
HALVES = 2


def harmonic(first, second):
    return 2.0 * first * second / (first + second)


def tile_of(plane, tile):
    start = plane * LAT * LAT + tile * LANES
    return slice(start, start + LANES)


def coefficients(sat_ref, head_ref, storage_ref, coef_ref):
    lane = lax.broadcasted_iota(jnp.int32, (8, LANES), 1)
    low = lane < LAT
    inside = lane % LAT != LAT - 1

    def wide(ref, plane, tile):
        return jnp.broadcast_to(ref[0:1, tile_of(plane, tile)], (8, LANES))

    conduct = [
        [wide(sat_ref, z, j) * jnp.exp(wide(head_ref, z, j)) for j in range(TILES)]
        for z in range(SLAB)
    ]
    for j in range(TILES):
        along_z = harmonic(conduct[0][j], conduct[1][j])
        for z in range(SLAB):
            own = conduct[z][j]
            right = jnp.where(inside, harmonic(own, pltpu.roll(own, LANES - 1, 1)), 0.0)
            left = pltpu.roll(right, 1, 1)
            within = harmonic(own, pltpu.roll(own, LAT, 1))
            before = pltpu.roll(conduct[z][max(j - 1, 0)], LAT, 1)
            after = pltpu.roll(conduct[z][min(j + 1, TILES - 1)], LAT, 1)
            across = harmonic(own, jnp.where(low, before, after))
            if j == 0:
                across = jnp.where(low, 0.0, across)
            if j == TILES - 1:
                across = jnp.where(low, across, 0.0)
            total = wide(storage_ref, z, j) + right + left + within + across + along_z
            for n, value in enumerate((total, right, left, within, across, along_z)):
                coef_ref[n, :, tile_of(z, j)] = value


def kernel(
    width,
    piece_rows,
    basis_ref,
    sat_ref,
    head_ref,
    storage_ref,
    counts_ref,
    partner_ref,
    owner_ref,
    diag_ref,
    face_ref,
    basis_v,
    image_v,
    coef_ref,
    face_src,
    face_recv,
    face_stage,
    face_fin,
    diag_src,
    diag_recv,
    diag_stage,
    diag_fin,
    inverse_ref,
    load_sem,
    face_sems,
    diag_sems,
):
    rows_total = basis_v.shape[0]
    pieces = rows_total // piece_rows
    stride = width // pieces
    half_rows = rows_total // HALVES
    me = lax.axis_index("wide")
    own_piece = me // stride
    is_middle = lax.rem(me, stride) == 0

    loads = []
    for h in range(HALVES):
        part = pl.ds(h * half_rows, half_rows)
        loads.append(
            pltpu.make_async_copy(basis_ref.at[0, part], basis_v.at[part], load_sem.at[h])
        )
        loads[-1].start()

    barrier = pltpu.get_barrier_semaphore()

    @pl.loop(1, width)
    def _(step):
        pl.semaphore_signal(
            barrier,
            inc=1,
            device_id={"wide": lax.rem(me + step, width)},
            device_id_type=pl.DeviceIdType.MESH,
        )

    coefficients(sat_ref, head_ref, storage_ref, coef_ref)

    @pl.loop(0, width)
    def _(d):
        found = jnp.int32(0)
        for i in range(width):
            found = jnp.where(owner_ref[i] == d, i, found)
        inverse_ref[d] = found

    pl.semaphore_wait(barrier, width - 1)

    own_count = counts_ref[me]
    lane = lax.broadcasted_iota(jnp.int32, (ROWS, LANES), 1)
    low = lane < LAT
    westerly = lane % LAT < 2

    def copy_to(src, dst, send_sem, recv_sem, target):
        return pltpu.make_async_remote_copy(
            src_ref=src,
            dst_ref=dst,
            send_sem=send_sem,
            recv_sem=recv_sem,
            device_id={"wide": target},
            device_id_type=pl.DeviceIdType.MESH,
        )

    def first_leg(src, recv, sems, piece):
        target = piece * stride
        return copy_to(
            src.at[piece], recv.at[me], sems.at[0, piece], sems.at[1, me], target
        )

    def second_leg(stage, fin, sems, target):
        return copy_to(
            stage.at[target],
            fin.at[own_piece],
            sems.at[2, target],
            sems.at[3, own_piece],
            target,
        )

    groups_per_piece = piece_rows // ROWS

    def group_rows(half, step):
        local_group = lax.rem(step + me * groups_per_piece, half_rows // ROWS)
        place = pl.multiple_of(local_group * ROWS, ROWS)
        return pl.multiple_of(half * half_rows + place, ROWS)

    def image_group(half, step):
        row = group_rows(half, step)
        values = {}
        turned = {}

        def value(z, j):
            if (z, j) not in values:
                values[z, j] = basis_v[pl.ds(row, ROWS), tile_of(z, j)].astype(jnp.float32)
            return values[z, j]

        def turn(z, j):
            j = min(max(j, 0), TILES - 1)
            if (z, j) not in turned:
                turned[z, j] = pltpu.roll(value(z, j), LAT, 1)
            return turned[z, j]

        def coef(n, z, j):
            one = coef_ref[n, :, tile_of(z, j)]
            return jnp.concatenate([one] * (ROWS // 8), axis=0)

        for j in range(TILES):
            along_z = coef(5, 0, j)
            for z in range(SLAB):
                own = value(z, j)
                image = coef(0, z, j) * own
                image = image - coef(1, z, j) * pltpu.roll(own, LANES - 1, 1)
                image = image - coef(2, z, j) * pltpu.roll(own, 1, 1)
                image = image - coef(3, z, j) * turn(z, j)
                image = image - coef(4, z, j) * jnp.where(low, turn(z, j - 1), turn(z, j + 1))
                image = image - along_z * value(1 - z, j)
                image_v[pl.ds(row, ROWS), tile_of(z, j)] = image.astype(jnp.bfloat16)

    def face_group(half, step):
        row = group_rows(half, step)
        keep = row + lax.broadcasted_iota(jnp.int32, (ROWS, LANES), 0) < own_count
        piece = row // piece_rows
        inner = pl.multiple_of(lax.rem(row, piece_rows), ROWS)
        for z in range(SLAB):
            for first in range(0, TILES, GROUP):
                held = None
                for j in range(first, first + GROUP):
                    shift = 4 * (j % GROUP)
                    landing = (lane - (LAT - 2) - shift + LANES) % LAT < 4
                    mixed = jnp.where(
                        westerly,
                        basis_v[pl.ds(row, ROWS), tile_of(z, j)].astype(jnp.float32),
                        image_v[pl.ds(row, ROWS), tile_of(z, j)].astype(jnp.float32),
                    )
                    if shift:
                        mixed = pltpu.roll(mixed, shift, 1)
                    held = mixed if held is None else jnp.where(landing, mixed, held)
                n = (z * TILES + first) // GROUP
                face_src[piece, pl.ds(inner, ROWS), n * LANES : (n + 1) * LANES] = jnp.where(
                    keep, held, 0.0
                ).astype(jnp.bfloat16)
        return piece

    def image_half(half):
        piece_per_half = pieces // HALVES

        @pl.loop(0, half_rows // ROWS)
        def _(step):
            image_group(half, step)

        @pl.loop(0, piece_per_half)
        def _(step):
            piece = None
            for part in range(groups_per_piece):
                piece = face_group(half, step * groups_per_piece + part)

            @pl.when(piece * stride != me)
            def _():
                first_leg(face_src, face_recv, face_sems, piece).start()

            @pl.when(piece * stride == me)
            def _():
                face_recv[me] = face_src[piece]

    def diag_whole():
        block = lax.dot_general(
            basis_v[...], image_v[...], (((1,), (1,)), ((), ())), preferred_element_type=jnp.float32
        )
        row = lax.broadcasted_iota(jnp.int32, block.shape, 0)
        column = lax.broadcasted_iota(jnp.int32, block.shape, 1)
        block = jnp.where((row < own_count) & (column < own_count), block, 0.0)
        diag_src[...] = block.astype(jnp.bfloat16).reshape(pieces, piece_rows, rows_total)

        @pl.loop(0, pieces)
        def _(step):
            piece = lax.rem(step + own_piece, pieces)

            @pl.when(piece * stride != me)
            def _():
                first_leg(diag_src, diag_recv, diag_sems, piece).start()

            @pl.when(piece * stride == me)
            def _():
                diag_recv[me] = diag_src[piece]

    def wait_first(src, recv, sems):
        @pl.loop(0, width)
        def _(source):
            @pl.when(source != me)
            def _():
                copy_to(
                    src.at[own_piece], recv.at[source], sems.at[0, own_piece], sems.at[1, source], source
                ).wait_recv()

    def wait_second(stage, fin, sems):
        @pl.loop(0, pieces)
        def _(piece):
            @pl.when(piece * stride != me)
            def _():
                copy_to(
                    stage.at[me], fin.at[piece], sems.at[2, me], sems.at[3, piece], piece * stride
                ).wait_recv()

    def forward(pick, src, recv, stage, fin, sems):
        @pl.when(is_middle)
        def _():
            wait_first(src, recv, sems)

            @pl.loop(1, width + 1)
            def _(step):
                target = lax.rem(me + step, width)
                taken = pick(inverse_ref[target])

                @pl.when(target != me)
                def _():
                    stage[target] = taken
                    second_leg(stage, fin, sems, target).start()

                @pl.when(target == me)
                def _():
                    fin[own_piece] = taken

    def wait_sent(src, recv, stage, fin, sems):
        @pl.loop(0, pieces)
        def _(piece):
            @pl.when(piece * stride != me)
            def _():
                first_leg(src, recv, sems, piece).wait_send()

        @pl.when(is_middle)
        def _():
            @pl.loop(0, width)
            def _(target):
                @pl.when(target != me)
                def _():
                    second_leg(stage, fin, sems, target).wait_send()

    face_lane = lax.broadcasted_iota(jnp.int32, (piece_rows, 2 * FACE), 1)
    easterly = face_lane % 4 >= 2

    def pick_face(source):
        east = face_recv[source].astype(jnp.float32)
        west = face_recv[partner_ref[source]].astype(jnp.float32)
        return jnp.where(easterly, east, west).astype(jnp.bfloat16)

    loads[0].wait()
    image_half(0)
    loads[1].wait()
    image_half(1)
    diag_whole()
    face_refs = (face_src, face_recv, face_stage, face_fin, face_sems)
    diag_refs = (diag_src, diag_recv, diag_stage, diag_fin, diag_sems)
    forward(pick_face, *face_refs)
    forward(lambda source: diag_recv[source], *diag_refs)
    wait_second(face_stage, face_fin, face_sems)
    face_ref[...] = face_fin[...].reshape(rows_total, 2 * FACE)
    wait_second(diag_stage, diag_fin, diag_sems)
    diag_ref[...] = diag_fin[...].reshape(rows_total, rows_total)
    wait_sent(*face_refs)
    wait_sent(*diag_refs)


def finish(diag_in, face_in, diag_ref, coupling_ref):
    diag_ref[0] = diag_in[...].astype(jnp.float32)
    easts, wests = [], []
    for n in range(2 * FACE // LANES):
        tile = face_in[:, n * LANES : (n + 1) * LANES].astype(jnp.float32)
        easterly = lax.broadcasted_iota(jnp.int32, tile.shape, 1) % 4 >= 2
        easts.append(jnp.where(easterly, tile, 0.0).astype(jnp.bfloat16))
        wests.append(pltpu.roll(tile, LAT - 2, 1).astype(jnp.bfloat16))
    coupling_ref[0] = lax.dot_general(
        jnp.concatenate(easts, axis=1),
        jnp.concatenate(wests, axis=1),
        (((1,), (1,)), ((), ())),
        preferred_element_type=jnp.float32,
    )


def local(width, basis, sat_cond, head, storage, counts, partner, owner):
    rows = basis.shape[1]
    cells = basis.shape[2]
    piece_rows = max(ROWS, rows // width)
    pieces = rows // piece_rows
    bf16 = jnp.bfloat16
    out = jax.ShapeDtypeStruct((1, rows, rows), jnp.float32)
    vmem = pl.BlockSpec(memory_space=pltpu.VMEM)
    smem = pl.BlockSpec(memory_space=pltpu.SMEM)
    diag, face = pl.pallas_call(
        functools.partial(kernel, width, piece_rows),
        out_shape=(
            jax.ShapeDtypeStruct((rows, rows), bf16),
            jax.ShapeDtypeStruct((rows, 2 * FACE), bf16),
        ),
        in_specs=[pl.BlockSpec(memory_space=pl.ANY), vmem, vmem, vmem, smem, smem, smem],
        out_specs=(vmem, vmem),
        scratch_shapes=[
            pltpu.VMEM((rows, cells), bf16),
            pltpu.VMEM((rows, cells), bf16),
            pltpu.VMEM((6, 8, cells), jnp.float32),
            pltpu.VMEM((pieces, piece_rows, 2 * FACE), bf16),
            pltpu.VMEM((width, piece_rows, 2 * FACE), bf16),
            pltpu.VMEM((width, piece_rows, 2 * FACE), bf16),
            pltpu.VMEM((pieces, piece_rows, 2 * FACE), bf16),
            pltpu.VMEM((pieces, piece_rows, rows), bf16),
            pltpu.VMEM((width, piece_rows, rows), bf16),
            pltpu.VMEM((width, piece_rows, rows), bf16),
            pltpu.VMEM((pieces, piece_rows, rows), bf16),
            pltpu.SMEM((width,), jnp.int32),
            pltpu.SemaphoreType.DMA((HALVES,)),
            pltpu.SemaphoreType.DMA((4, width)),
            pltpu.SemaphoreType.DMA((4, width)),
        ],
        compiler_params=pltpu.CompilerParams(
            collective_id=0, has_side_effects=True, vmem_limit_bytes=60 * 1024 * 1024
        ),
    )(basis, sat_cond, head, storage, counts, partner, owner)
    return pl.pallas_call(
        finish, out_shape=(out, out), in_specs=[vmem, vmem], out_specs=(vmem, vmem)
    )(diag, face)


def solution(mesh):
    placed = (
        P(("group", "wide"), None, None),
        P(("group", "wide"), None),
        P(("group", "wide"), None),
        P(("group", "wide"), None),
        P("group"),
        P("group"),
        P("group"),
    )
    return jax.shard_map(
        functools.partial(local, mesh.shape["wide"]),
        mesh=mesh,
        in_specs=placed,
        out_specs=(P(("group", "wide"), None, None), P(("group", "wide"), None, None)),
        check_vma=False,
    )
```

```python
import functools

import jax
import jax.numpy as jnp
from jax import lax
from jax.experimental import pallas as pl
from jax.experimental.pallas import tpu as pltpu
from jax.sharding import PartitionSpec as P

LAT = 64
SLAB = 2
FACE = 256
LANES = 128
ROWS = 16
IMAGE_ROWS = 32
TILES = LAT * LAT // LANES
GROUP = 16
HALVES = 2


def harmonic(first, second):
    return 2.0 * first * second / (first + second)


def tile_of(plane, tile):
    start = plane * LAT * LAT + tile * LANES
    return slice(start, start + LANES)


def coefficients(sat_ref, head_ref, storage_ref, coef_ref):
    lane = lax.broadcasted_iota(jnp.int32, (8, LANES), 1)
    low = lane < LAT
    inside = lane % LAT != LAT - 1

    def wide(ref, plane, tile):
        return jnp.broadcast_to(ref[0:1, tile_of(plane, tile)], (8, LANES))

    conduct = [
        [wide(sat_ref, z, j) * jnp.exp(wide(head_ref, z, j)) for j in range(TILES)]
        for z in range(SLAB)
    ]
    for j in range(TILES):
        along_z = harmonic(conduct[0][j], conduct[1][j])
        for z in range(SLAB):
            own = conduct[z][j]
            right = jnp.where(inside, harmonic(own, pltpu.roll(own, LANES - 1, 1)), 0.0)
            left = pltpu.roll(right, 1, 1)
            within = harmonic(own, pltpu.roll(own, LAT, 1))
            before = pltpu.roll(conduct[z][max(j - 1, 0)], LAT, 1)
            after = pltpu.roll(conduct[z][min(j + 1, TILES - 1)], LAT, 1)
            across = harmonic(own, jnp.where(low, before, after))
            if j == 0:
                across = jnp.where(low, 0.0, across)
            if j == TILES - 1:
                across = jnp.where(low, across, 0.0)
            total = wide(storage_ref, z, j) + right + left + within + across + along_z
            for n, value in enumerate((total, right, left, within, across, along_z)):
                coef_ref[n, :, tile_of(z, j)] = value


def kernel(
    width,
    piece_rows,
    basis_ref,
    sat_ref,
    head_ref,
    storage_ref,
    counts_ref,
    partner_ref,
    owner_ref,
    diag_ref,
    face_ref,
    basis_v,
    image_v,
    coef_ref,
    face_src,
    face_recv,
    face_stage,
    face_fin,
    diag_src,
    diag_recv,
    diag_stage,
    diag_fin,
    inverse_ref,
    load_sem,
    face_sems,
    diag_sems,
):
    rows_total = basis_v.shape[0]
    pieces = rows_total // piece_rows
    stride = width // pieces
    half_rows = rows_total // HALVES
    me = lax.axis_index("wide")
    own_piece = me // stride
    is_middle = lax.rem(me, stride) == 0

    loads = []
    for h in range(HALVES):
        part = pl.ds(h * half_rows, half_rows)
        loads.append(
            pltpu.make_async_copy(basis_ref.at[0, part], basis_v.at[part], load_sem.at[h])
        )
        loads[-1].start()

    barrier = pltpu.get_barrier_semaphore()

    @pl.loop(1, width)
    def _(step):
        pl.semaphore_signal(
            barrier,
            inc=1,
            device_id={"wide": lax.rem(me + step, width)},
            device_id_type=pl.DeviceIdType.MESH,
        )

    coefficients(sat_ref, head_ref, storage_ref, coef_ref)

    @pl.loop(0, width)
    def _(d):
        found = jnp.int32(0)
        for i in range(width):
            found = jnp.where(owner_ref[i] == d, i, found)
        inverse_ref[d] = found

    pl.semaphore_wait(barrier, width - 1)

    own_count = counts_ref[me]
    lane = lax.broadcasted_iota(jnp.int32, (ROWS, LANES), 1)
    westerly = lane % LAT < 2

    def copy_to(src, dst, send_sem, recv_sem, target):
        return pltpu.make_async_remote_copy(
            src_ref=src,
            dst_ref=dst,
            send_sem=send_sem,
            recv_sem=recv_sem,
            device_id={"wide": target},
            device_id_type=pl.DeviceIdType.MESH,
        )

    def first_leg(src, recv, sems, piece):
        target = piece * stride
        return copy_to(
            src.at[piece], recv.at[me], sems.at[0, piece], sems.at[1, me], target
        )

    def second_leg(stage, fin, sems, target):
        return copy_to(
            stage.at[target],
            fin.at[own_piece],
            sems.at[2, target],
            sems.at[3, own_piece],
            target,
        )

    groups_per_piece = piece_rows // ROWS

    def group_rows(half, step):
        local_group = lax.rem(step + me * groups_per_piece, half_rows // ROWS)
        place = pl.multiple_of(local_group * ROWS, ROWS)
        return pl.multiple_of(half * half_rows + place, ROWS)

    def image_group(half, step):
        row = pl.multiple_of(half * half_rows + step * IMAGE_ROWS, IMAGE_ROWS)
        low_half = lax.broadcasted_iota(jnp.int32, (IMAGE_ROWS, LANES), 1) < LAT
        values = {}
        turned = {}

        def value(z, j):
            if (z, j) not in values:
                values[z, j] = basis_v[pl.ds(row, IMAGE_ROWS), tile_of(z, j)].astype(jnp.float32)
            return values[z, j]

        def turn(z, j):
            j = min(max(j, 0), TILES - 1)
            if (z, j) not in turned:
                turned[z, j] = pltpu.roll(value(z, j), LAT, 1)
            return turned[z, j]

        def coef(n, z, j):
            one = coef_ref[n, :, tile_of(z, j)]
            return jnp.concatenate([one] * (IMAGE_ROWS // 8), axis=0)

        for j in range(TILES):
            along_z = coef(5, 0, j)
            for z in range(SLAB):
                own = value(z, j)
                image = coef(0, z, j) * own
                image = image - coef(1, z, j) * pltpu.roll(own, LANES - 1, 1)
                image = image - coef(2, z, j) * pltpu.roll(own, 1, 1)
                image = image - coef(3, z, j) * turn(z, j)
                image = image - coef(4, z, j) * jnp.where(low_half, turn(z, j - 1), turn(z, j + 1))
                image = image - along_z * value(1 - z, j)
                image_v[pl.ds(row, IMAGE_ROWS), tile_of(z, j)] = image.astype(jnp.bfloat16)

    def face_group(half, step):
        row = group_rows(half, step)
        keep = row + lax.broadcasted_iota(jnp.int32, (ROWS, LANES), 0) < own_count
        piece = row // piece_rows
        inner = pl.multiple_of(lax.rem(row, piece_rows), ROWS)
        for z in range(SLAB):
            for first in range(0, TILES, GROUP):
                held = None
                for j in range(first, first + GROUP):
                    shift = 4 * (j % GROUP)
                    landing = (lane - (LAT - 2) - shift + LANES) % LAT < 4
                    mixed = jnp.where(
                        westerly,
                        basis_v[pl.ds(row, ROWS), tile_of(z, j)].astype(jnp.float32),
                        image_v[pl.ds(row, ROWS), tile_of(z, j)].astype(jnp.float32),
                    )
                    if shift:
                        mixed = pltpu.roll(mixed, shift, 1)
                    held = mixed if held is None else jnp.where(landing, mixed, held)
                n = (z * TILES + first) // GROUP
                face_src[piece, pl.ds(inner, ROWS), n * LANES : (n + 1) * LANES] = jnp.where(
                    keep, held, 0.0
                ).astype(jnp.bfloat16)
        return piece

    def image_half(half):
        piece_per_half = pieces // HALVES

        @pl.loop(0, half_rows // IMAGE_ROWS)
        def _(step):
            image_group(half, step)

        @pl.loop(0, piece_per_half)
        def _(step):
            piece = None
            for part in range(groups_per_piece):
                piece = face_group(half, step * groups_per_piece + part)

            @pl.when(piece * stride != me)
            def _():
                first_leg(face_src, face_recv, face_sems, piece).start()

            @pl.when(piece * stride == me)
            def _():
                face_recv[me] = face_src[piece]

    def diag_whole():
        block = lax.dot_general(
            basis_v[...], image_v[...], (((1,), (1,)), ((), ())), preferred_element_type=jnp.float32
        )
        row = lax.broadcasted_iota(jnp.int32, block.shape, 0)
        column = lax.broadcasted_iota(jnp.int32, block.shape, 1)
        block = jnp.where((row < own_count) & (column < own_count), block, 0.0)
        diag_src[...] = block.astype(jnp.bfloat16).reshape(pieces, piece_rows, rows_total)

        @pl.loop(0, pieces)
        def _(step):
            piece = lax.rem(step + own_piece, pieces)

            @pl.when(piece * stride != me)
            def _():
                first_leg(diag_src, diag_recv, diag_sems, piece).start()

            @pl.when(piece * stride == me)
            def _():
                diag_recv[me] = diag_src[piece]

    def wait_first(src, recv, sems):
        @pl.loop(0, width)
        def _(source):
            @pl.when(source != me)
            def _():
                copy_to(
                    src.at[own_piece], recv.at[source], sems.at[0, own_piece], sems.at[1, source], source
                ).wait_recv()

    def wait_second(stage, fin, sems):
        @pl.loop(0, pieces)
        def _(piece):
            @pl.when(piece * stride != me)
            def _():
                copy_to(
                    stage.at[me], fin.at[piece], sems.at[2, me], sems.at[3, piece], piece * stride
                ).wait_recv()

    def forward(pick, src, recv, stage, fin, sems):
        @pl.when(is_middle)
        def _():
            wait_first(src, recv, sems)

            @pl.loop(1, width + 1)
            def _(step):
                target = lax.rem(me + step, width)
                taken = pick(inverse_ref[target])

                @pl.when(target != me)
                def _():
                    stage[target] = taken
                    second_leg(stage, fin, sems, target).start()

                @pl.when(target == me)
                def _():
                    fin[own_piece] = taken

    def wait_sent(src, recv, stage, fin, sems):
        @pl.loop(0, pieces)
        def _(piece):
            @pl.when(piece * stride != me)
            def _():
                first_leg(src, recv, sems, piece).wait_send()

        @pl.when(is_middle)
        def _():
            @pl.loop(0, width)
            def _(target):
                @pl.when(target != me)
                def _():
                    second_leg(stage, fin, sems, target).wait_send()

    face_lane = lax.broadcasted_iota(jnp.int32, (piece_rows, 2 * FACE), 1)
    easterly = face_lane % 4 >= 2

    def pick_face(source):
        east = face_recv[source].astype(jnp.float32)
        west = face_recv[partner_ref[source]].astype(jnp.float32)
        return jnp.where(easterly, east, west).astype(jnp.bfloat16)

    loads[0].wait()
    image_half(0)
    loads[1].wait()
    image_half(1)
    diag_whole()
    face_refs = (face_src, face_recv, face_stage, face_fin, face_sems)
    diag_refs = (diag_src, diag_recv, diag_stage, diag_fin, diag_sems)
    forward(pick_face, *face_refs)
    forward(lambda source: diag_recv[source], *diag_refs)
    wait_second(face_stage, face_fin, face_sems)
    face_ref[...] = face_fin[...].reshape(rows_total, 2 * FACE)
    wait_second(diag_stage, diag_fin, diag_sems)
    diag_ref[...] = diag_fin[...].reshape(rows_total, rows_total)
    wait_sent(*face_refs)
    wait_sent(*diag_refs)


def finish(diag_in, face_in, diag_ref, coupling_ref):
    diag_ref[0] = diag_in[...].astype(jnp.float32)
    easts, wests = [], []
    for n in range(2 * FACE // LANES):
        tile = face_in[:, n * LANES : (n + 1) * LANES].astype(jnp.float32)
        easterly = lax.broadcasted_iota(jnp.int32, tile.shape, 1) % 4 >= 2
        easts.append(jnp.where(easterly, tile, 0.0).astype(jnp.bfloat16))
        wests.append(pltpu.roll(tile, LAT - 2, 1).astype(jnp.bfloat16))
    coupling_ref[0] = lax.dot_general(
        jnp.concatenate(easts, axis=1),
        jnp.concatenate(wests, axis=1),
        (((1,), (1,)), ((), ())),
        preferred_element_type=jnp.float32,
    )


def local(width, basis, sat_cond, head, storage, counts, partner, owner):
    rows = basis.shape[1]
    cells = basis.shape[2]
    piece_rows = max(ROWS, rows // width)
    pieces = rows // piece_rows
    bf16 = jnp.bfloat16
    out = jax.ShapeDtypeStruct((1, rows, rows), jnp.float32)
    vmem = pl.BlockSpec(memory_space=pltpu.VMEM)
    smem = pl.BlockSpec(memory_space=pltpu.SMEM)
    diag, face = pl.pallas_call(
        functools.partial(kernel, width, piece_rows),
        out_shape=(
            jax.ShapeDtypeStruct((rows, rows), bf16),
            jax.ShapeDtypeStruct((rows, 2 * FACE), bf16),
        ),
        in_specs=[pl.BlockSpec(memory_space=pl.ANY), vmem, vmem, vmem, smem, smem, smem],
        out_specs=(vmem, vmem),
        scratch_shapes=[
            pltpu.VMEM((rows, cells), bf16),
            pltpu.VMEM((rows, cells), bf16),
            pltpu.VMEM((6, 8, cells), jnp.float32),
            pltpu.VMEM((pieces, piece_rows, 2 * FACE), bf16),
            pltpu.VMEM((width, piece_rows, 2 * FACE), bf16),
            pltpu.VMEM((width, piece_rows, 2 * FACE), bf16),
            pltpu.VMEM((pieces, piece_rows, 2 * FACE), bf16),
            pltpu.VMEM((pieces, piece_rows, rows), bf16),
            pltpu.VMEM((width, piece_rows, rows), bf16),
            pltpu.VMEM((width, piece_rows, rows), bf16),
            pltpu.VMEM((pieces, piece_rows, rows), bf16),
            pltpu.SMEM((width,), jnp.int32),
            pltpu.SemaphoreType.DMA((HALVES,)),
            pltpu.SemaphoreType.DMA((4, width)),
            pltpu.SemaphoreType.DMA((4, width)),
        ],
        compiler_params=pltpu.CompilerParams(
            collective_id=0, has_side_effects=True, vmem_limit_bytes=60 * 1024 * 1024
        ),
    )(basis, sat_cond, head, storage, counts, partner, owner)
    return pl.pallas_call(
        finish, out_shape=(out, out), in_specs=[vmem, vmem], out_specs=(vmem, vmem)
    )(diag, face)


def solution(mesh):
    placed = (
        P(("group", "wide"), None, None),
        P(("group", "wide"), None),
        P(("group", "wide"), None),
        P(("group", "wide"), None),
        P("group"),
        P("group"),
        P("group"),
    )
    return jax.shard_map(
        functools.partial(local, mesh.shape["wide"]),
        mesh=mesh,
        in_specs=placed,
        out_specs=(P(("group", "wide"), None, None), P(("group", "wide"), None, None)),
        check_vma=False,
    )
```
